32 devices in a mesh: parts: 2 (over x), blk: 8 (over z, y), clus: 2 (over core).
Axes of the slice: x: 2, y: 2, z: 4, core: 2. Of those that a mesh axis runs over, the one named last changes fastest.
Arguments:
- embeddings: bfloat16 [16384, 1024], P(('parts', 'blk', 'clus')), parts along dimension 0, as said below
- assignment: int32 [16384, 1], P(('parts', 'blk', 'clus')), parts along dimension 0, may hold values from 0 to 15; in each aligned block of 512 rows (0 to 511, 512 to 1023, ...) at most 128 rows name the same one
Outputs:
- prune_score: float32 [16384], P(('parts', 'blk', 'clus')), parts along dimension 0
The draws below stay inside these ranges and needn't reach their ends.
There are 2 independent parts, one for each index of `parts`. The reference program is written for one: setup_inputs(seed, part) draws one part's arguments, and reference() takes and returns one part's arrays. A program takes and returns all parts, laid end to end along the dimension named above; each array names one. Nothing has to cross between parts.
Inputs may be any that keep to these rules, and one draw needn't show every extreme that they name: `assignment`: each document names one cluster; among the documents of one device no cluster is named by more than 128, and every cluster is named by some document. Real-valued embeddings; no row is zero.
All inputs are finite; a program needn't handle non-finite values.
Results may differ from the reference program's by a relative error of at most 0.0003.
Values may be sent and summed in bfloat16 or wider, within the bound.
A program may use at most 64 MiB of HBM per device.

```python
import math
import jax
import jax.numpy as jnp
import numpy as np
from jax import lax

D = 1024
TOK = 512
NCL = 16
CAP = 128
ROWS = 8192


def draw_embeddings(key, part):
    key = jax.random.fold_in(key, 7)
    key_topic, key_pick, key_weight, key_scale, key_noise = jax.random.split(key, 5)
    topic_count = max(D // 4, 8)
    topics = jax.random.normal(key_topic, (topic_count, D), jnp.float32)
    pick = jax.random.randint(key_pick, (ROWS,), 0, topic_count)
    chosen = topics[pick]
    strength = jnp.exp(jax.random.uniform(key_weight, (ROWS, 1), jnp.float32, jnp.log(1.2), jnp.log(3.2)))
    scales = jnp.exp(jax.random.uniform(key_scale, (ROWS, 1), jnp.float32, jnp.log(0.2), jnp.log(2.0)))
    noise = jax.random.normal(key_noise, (ROWS, D), jnp.float32)
    result = (noise + strength * chosen) * scales
    return result.astype(jnp.bfloat16)


def deal_out(rng, own, number, rows, amount, top, limit, skew):
    ranking = jax.random.permutation(rng, amount)
    heavy_load, ordinary = shares(amount, rows * top, limit, skew, True), shares(amount, rows * top, limit, skew, False)
    places = jnp.arange(amount)

    def named(lengths, rotation):
        used = int((lengths > 0).sum())
        fixed = max(1, used // 4)
        shifted = fixed + (places - fixed + rotation * (used - fixed)) % max(1, amount - fixed)
        return jnp.zeros((amount,), jnp.int32).at[ranking[jnp.where(places < fixed, places, shifted)]].set(jnp.asarray(lengths, jnp.int32))

    lengths = jnp.where(number % 4 == 0, named(heavy_load, number // 4), named(ordinary, number - number // 4 - 1))
    mixed = jax.random.permutation(jax.random.fold_in(own, 3), amount)
    donor, taker = mixed[0:amount // 2 * 2:2], mixed[1:amount // 2 * 2:2]
    margin = jnp.minimum(lengths[donor] - 1, limit - lengths[taker]) // 2
    margin = jnp.where((donor == ranking[0]) | (taker == ranking[0]) | (lengths[taker] == 0), 0, jnp.maximum(margin, 0))
    shifted = jax.random.randint(jax.random.fold_in(own, 4), (amount // 2,), 0, 1 << 20) % (margin + 1)
    lengths = lengths.at[donor].add(-shifted).at[taker].add(shifted)
    labels = jnp.searchsorted(jnp.cumsum(lengths), jnp.arange(rows * top), side="right").astype(jnp.int32)
    listing = labels.reshape(top, rows).T
    listing = listing[jax.random.permutation(jax.random.fold_in(own, 1), rows)]
    rotation = jax.random.randint(jax.random.fold_in(own, 2), (rows, 1), 0, top)
    return jnp.take_along_axis(listing, (jnp.arange(top)[None, :] + rotation) % top, axis=1)


def shares(number_of, total, bound, lean, full):
    loads = [(1 << 20) // math.isqrt(rank ** lean) + 1 for rank in range(1, number_of + 1)]
    largest = bound if full else min(bound, max(-(-total // number_of), total * loads[0] // sum(loads)))
    least = 1 if total - largest >= number_of - 1 else 0
    holding, rest = [largest] + [least] * (number_of - 1), total - largest - least * (number_of - 1)
    while rest > 0:
        free = [i for i in range(1, number_of) if holding[i] < largest] or [i for i in range(1, number_of) if holding[i] < bound]
        mass, left = sum([loads[i] for i in free]), rest
        for i in free:
            extra = min(bound - holding[i], max(1, left * loads[i] // mass), rest)
            holding[i] = holding[i] + extra
            rest = rest - extra
    return np.array(holding)


def setup_inputs(seed: int = 0, part: int = 0) -> dict:
    key_of = jax.random.split(jax.random.key(seed), 3)
    part_splits = jax.random.split(jax.random.fold_in(key_of[2], part), 3)
    embeddings = draw_embeddings(jax.random.fold_in(jax.random.fold_in(key_of[2], part), 71), part)
    assignment_keys = jax.random.split(jax.random.fold_in(part_splits[1], 1), ROWS // TOK)
    assignment_turns = jax.random.permutation(jax.random.fold_in(part_splits[1], 3), ROWS // TOK)
    assignment = jax.vmap(lambda own, number: deal_out(jax.random.fold_in(part_splits[1], 2), own, number, TOK, NCL, 1, CAP, 2))(assignment_keys, assignment_turns).reshape((ROWS, 1))
    return {"embeddings": embeddings, "assignment": assignment}


kernel_scale = 4.0

def unit_rows(embeddings):
    widened = embeddings.astype(jnp.float32)
    normed = widened * lax.rsqrt(lax.optimization_barrier(jnp.mean(widened * widened, axis=1, keepdims=True)) + 1e-06) * embeddings.shape[1] ** (-0.5)
    return normed.astype(jnp.bfloat16)

def reference(embeddings, assignment):
    buffer_rows = NCL * CAP
    unit = unit_rows(embeddings)
    cluster = assignment[:, 0].astype(jnp.int32)
    order = jnp.argsort(cluster, stable=True).astype(jnp.int32)
    sorted_rows = jnp.concatenate([unit[order], jnp.zeros((buffer_rows, D), jnp.bfloat16)], axis=0)
    counts = lax.optimization_barrier(jnp.sum((cluster[:, None] == jnp.arange(NCL, dtype=jnp.int32)[None, :]).astype(jnp.int32), axis=0)).astype(jnp.int32)
    starts = (jnp.cumsum(counts) - counts).astype(jnp.int32)

    def per_cluster(index):
        segment = lax.dynamic_slice_in_dim(sorted_rows, starts[index], buffer_rows, 0).astype(jnp.float32)
        gram = jnp.dot(segment, segment.T, precision=lax.Precision.HIGHEST, preferred_element_type=jnp.float32)
        alive_mask = (jnp.arange(buffer_rows, dtype=jnp.int32) < counts[index]).astype(jnp.float32)
        density = lax.optimization_barrier(jnp.sum(jnp.exp(kernel_scale * (gram - 1.0)) * alive_mask[None, :], axis=1))
        return jnp.log(density / counts[index].astype(jnp.float32))
    table = lax.map(per_cluster, jnp.arange(NCL, dtype=jnp.int32))
    sorted_cluster = cluster[order]
    offsets = (jnp.arange(ROWS, dtype=jnp.int32) - starts[sorted_cluster]).astype(jnp.int32)
    sorted_score = table[sorted_cluster, offsets]
    return jnp.zeros((ROWS,), jnp.float32).at[order].set(sorted_score)
```

```python
import functools

import jax
import jax.numpy as jnp
from jax import lax
from jax.experimental import pallas as pl
from jax.experimental.pallas import tpu as pltpu
from jax.sharding import PartitionSpec as P

kernel_scale = 4.0
MESH = pl.DeviceIdType.MESH
CHUNKS = 4
HALF = 256
LANES = 128


def unit_rows(embeddings):
    widened = embeddings.astype(jnp.float32)
    normed = (
        widened
        * lax.rsqrt(jnp.mean(widened * widened, axis=1, keepdims=True) + 1e-06)
        * embeddings.shape[1] ** (-0.5)
    )
    return normed.astype(jnp.bfloat16)


def pair_kernel(
    emb_ref, id_ref, out_ref,
    line, plane, ids, id_cols, row_acc, line_part, plane_part, gathered,
    line_send, line_recv, plane_send, plane_recv, id_send, id_recv, part_send, part_recv,
):
    tok, width = emb_ref.shape
    rows = tok // CHUNKS
    part, blk, core = lax.axis_index("parts"), lax.axis_index("blk"), lax.axis_index("clus")
    z, y = blk // 2, blk % 2
    flip = 1 - 2 * part
    level = 3 * part + flip * z
    me = blk * 2 + core
    spot = y * 2 + core

    def at_level(other, oy=None, ocore=None):
        oz = 3 * part + flip * other
        return (part, oz * 2 + (y if oy is None else oy), core if ocore is None else ocore)

    def span(c):
        return pl.ds(pl.multiple_of(c * rows, rows), rows)

    def line_copy(source, c, target):
        return pltpu.make_async_remote_copy(
            src_ref=line.at[source, span(c)], dst_ref=line.at[source, span(c)],
            send_sem=line_send.at[source, c], recv_sem=line_recv.at[source, c],
            device_id=at_level(target), device_id_type=MESH)

    def plane_copy(kind, slot, c, target):
        return pltpu.make_async_remote_copy(
            src_ref=plane.at[slot, span(c)], dst_ref=plane.at[slot, span(c)],
            send_sem=plane_send.at[kind, c], recv_sem=plane_recv.at[slot, c],
            device_id=target, device_id_type=MESH)

    y_peer = at_level(level, oy=1 - y)
    c_peer = at_level(level, ocore=1 - core)
    y_spot = (1 - y) * 2 + core
    c_spot = y * 2 + 1 - core
    d_spot = (1 - y) * 2 + 1 - core
    sends = ((level == 0) | (level == 1) | (level == 3))
    target = jnp.where(level == 3, 2, level + 1)

    barrier = pltpu.get_barrier_semaphore()

    def other(k):
        dev = (me + k) % 16
        return dev, (part, dev // 2, dev % 2)

    @pl.loop(1, 16)
    def _(k):
        pl.semaphore_signal(barrier, inc=1, device_id=other(k)[1], device_id_type=MESH)

    ids[me] = id_ref[...]
    row_acc[...] = jnp.zeros_like(row_acc)
    pl.semaphore_wait(barrier, 15)

    def id_copy(dev, at):
        return pltpu.make_async_remote_copy(
            src_ref=ids.at[me], dst_ref=ids.at[me],
            send_sem=id_send.at[dev], recv_sem=id_recv.at[me],
            device_id=at, device_id_type=MESH)

    def id_arrival(dev):
        return pltpu.make_async_remote_copy(
            src_ref=ids.at[dev], dst_ref=ids.at[dev],
            send_sem=id_send.at[dev], recv_sem=id_recv.at[dev],
            device_id=other(1)[1], device_id_type=MESH)

    @pl.loop(0, CHUNKS)
    def _(c):
        unit = unit_rows(emb_ref[span(c), :])
        line[level, span(c)] = unit
        plane[spot, span(c)] = unit

        @pl.when(sends)
        def _():
            line_copy(level, c, target).start()
        plane_copy(0, spot, c, y_peer).start()
        plane_copy(1, spot, c, c_peer).start()

    @pl.loop(1, 16)
    def _(k):
        dev, at = other(k)
        id_copy(dev, at).start()

    @pl.loop(1, 16)
    def _(k):
        id_arrival(other(k)[0]).wait_recv()

    @pl.loop(0, 4)
    def _(b):
        row = jnp.broadcast_to(ids[(blk - y) * 2 + b], (LANES, tok))
        id_cols[b] = row.T

    own_ids = id_ref[...]

    def count_cluster(d, total):
        col = jnp.broadcast_to(ids[d], (LANES, tok)).T
        parts = []
        for s in range(tok // LANES):
            same = col == own_ids[:, s * LANES:(s + 1) * LANES]
            parts.append(jnp.sum(jnp.where(same, 1.0, 0.0), axis=0, keepdims=True))
        return total + jnp.concatenate(parts, axis=1)

    count = lax.fori_loop(0, 16, count_cluster, jnp.zeros((1, tok), jnp.float32))

    @pl.loop(0, CHUNKS)
    def _(c):
        plane_copy(0, y_spot, c, y_peer).wait_recv()
        plane_copy(2, y_spot, c, c_peer).start()

        @pl.when((level == 1) | (level == 2))
        def _():
            line_copy(level - 1, c, target).wait_recv()
            line_copy(level - 1, c, level + 1).start()

    @pl.loop(0, CHUNKS)
    def _(c):
        plane_copy(1, c_spot, c, c_peer).wait_recv()
        plane_copy(2, d_spot, c, c_peer).wait_recv()

    steps = jnp.where(level == 0, 1, jnp.where(level == 1, 2, jnp.where(level == 2, 4, 3)))

    def source_of(t):
        at_two = jnp.where(t == 1, 1, jnp.where(t == 2, 3, 0))
        at_three = jnp.where(t == 1, 1, 0)
        later = jnp.where(level == 2, at_two, jnp.where(level == 3, at_three, 0))
        return jnp.where(t == 0, level, later)

    def part_copy(buffer, slot, sem, at):
        return pltpu.make_async_remote_copy(
            src_ref=buffer.at[slot], dst_ref=gathered.at[me],
            send_sem=part_send.at[sem], recv_sem=part_recv.at[me],
            device_id=at, device_id_type=MESH)

    @pl.loop(0, steps)
    def _(t):
        source = source_of(t)
        own = t == 0

        @pl.when(level == 2)
        def _():
            line_copy(0, t, target).wait_recv()
            line_copy(0, t, 3).start()

        src_dev = (3 * part + flip * source) * 4 + spot
        for h in range(tok // HALF):
            @pl.when(((level == 3) & (t > 0)) | ((level == 2) & (t == 2)))
            def _():
                for c in range(h * HALF // rows, (h + 1) * HALF // rows):
                    line_copy(source, c, target).wait_recv()

            id_row = ids[src_dev][:, h * HALF:(h + 1) * HALF]

            def meet(b, total):
                block = line[source, h * HALF:(h + 1) * HALF, :]
                gram = lax.dot_general(
                    plane[b], block, (((1,), (1,)), ((), ())),
                    preferred_element_type=jnp.float32)
                value = jnp.exp(kernel_scale * (gram - 1.0))
                col = id_cols[b]
                sums, rowsum = [], None
                for s in range(HALF // LANES):
                    lanes = slice(s * LANES, (s + 1) * LANES)
                    kept = jnp.where(col == id_row[:, lanes], value[:, lanes], 0.0)
                    sums.append(jnp.sum(kept, axis=0, keepdims=True))
                    rowsum = kept if rowsum is None else rowsum + kept

                @pl.when(t > 0)
                def _():
                    row_acc[b] = row_acc[b] + rowsum
                return total + jnp.concatenate(sums, axis=1)

            line_part[source, :, h * HALF:(h + 1) * HALF] = lax.fori_loop(
                0, 4, meet, jnp.zeros((1, HALF), jnp.float32))

        @pl.when(t > 0)
        def _():
            part_copy(line_part, source, source, at_level(source)).start()

    def plane_peer(k):
        peer = (spot + k) % 4
        return peer, at_level(level, oy=peer // 2, ocore=peer % 2)

    @pl.when(level > 0)
    def _():
        for b in range(4):
            plane_part[b] = jnp.sum(row_acc[b].T, axis=0, keepdims=True)
        for k in range(1, 4):
            peer, at = plane_peer(k)
            part_copy(plane_part, peer, 4 + peer, at).start()

    total = line_part[level]
    out_ref[...] = total

    def part_arrival(dev):
        return pltpu.make_async_remote_copy(
            src_ref=line_part.at[0], dst_ref=gathered.at[dev],
            send_sem=part_send.at[0], recv_sem=part_recv.at[dev],
            device_id=y_peer, device_id_type=MESH)

    def take(source_level):
        dev = (3 * part + flip * source_level) * 4 + spot
        part_arrival(dev).wait_recv()
        out_ref[...] = out_ref[...] + gathered[dev]

    @pl.when(level == 0)
    def _():
        take(1)

    @pl.when((level != 2))
    def _():
        take(2)

    @pl.when(level < 2)
    def _():
        take(3)

    @pl.when(level > 0)
    def _():
        out_ref[...] = out_ref[...] + plane_part[spot]
        for k in range(1, 4):
            dev = (blk - y) * 2 + plane_peer(k)[0]
            part_arrival(dev).wait_recv()
            out_ref[...] = out_ref[...] + gathered[dev]

    out_ref[...] = jnp.log(out_ref[...] / count)

    @pl.loop(1, 16)
    def _(k):
        dev, at = other(k)
        id_copy(dev, at).wait_send()

    @pl.loop(0, CHUNKS)
    def _(c):
        @pl.when(sends)
        def _():
            line_copy(level, c, target).wait_send()

        @pl.when((level == 1) | (level == 2))
        def _():
            line_copy(level - 1, c, target).wait_send()

        @pl.when(level == 2)
        def _():
            line_copy(0, c, target).wait_send()
        plane_copy(0, spot, c, y_peer).wait_send()
        plane_copy(1, spot, c, c_peer).wait_send()
        plane_copy(2, y_spot, c, c_peer).wait_send()

    @pl.loop(1, steps)
    def _(t):
        source = source_of(t)
        part_copy(line_part, source, source, at_level(source)).wait_send()

    @pl.when(level > 0)
    def _():
        for k in range(1, 4):
            peer, at = plane_peer(k)
            part_copy(plane_part, peer, 4 + peer, at).wait_send()


def pair_scores(embeddings, assignment):
    tok, width = embeddings.shape
    score = pl.pallas_call(
        pair_kernel,
        out_shape=jax.ShapeDtypeStruct((1, tok), jnp.float32),
        in_specs=[pl.BlockSpec(memory_space=pltpu.VMEM)] * 2,
        out_specs=pl.BlockSpec(memory_space=pltpu.VMEM),
        scratch_shapes=[
            pltpu.VMEM((4, tok, width), jnp.bfloat16),
            pltpu.VMEM((4, tok, width), jnp.bfloat16),
            pltpu.VMEM((16, 1, tok), jnp.int32),
            pltpu.VMEM((4, tok, LANES), jnp.int32),
            pltpu.VMEM((4, tok, LANES), jnp.float32),
            pltpu.VMEM((4, 1, tok), jnp.float32),
            pltpu.VMEM((4, 1, tok), jnp.float32),
            pltpu.VMEM((16, 1, tok), jnp.float32),
            pltpu.SemaphoreType.DMA((4, CHUNKS)),
            pltpu.SemaphoreType.DMA((4, CHUNKS)),
            pltpu.SemaphoreType.DMA((3, CHUNKS)),
            pltpu.SemaphoreType.DMA((4, CHUNKS)),
            pltpu.SemaphoreType.DMA((16,)),
            pltpu.SemaphoreType.DMA((16,)),
            pltpu.SemaphoreType.DMA((8,)),
            pltpu.SemaphoreType.DMA((16,)),
        ],
        compiler_params=pltpu.CompilerParams(
            collective_id=0, has_side_effects=True, vmem_limit_bytes=40 << 20),
    )(embeddings, assignment.reshape(1, tok))
    return score.reshape(tok)


def tile_density(queries, keys, key_weight):
    gram = lax.dot_general(
        queries, keys, (((1,), (1,)), ((), ())), preferred_element_type=jnp.float32
    )
    return jnp.sum(jnp.exp(kernel_scale * (gram - 1.0)) * key_weight[None, :], axis=1)


def routed_scores(embeddings, assignment):
    local_rows = embeddings.shape[0]
    feature_width = embeddings.shape[1]
    owners = lax.axis_size(("blk", "clus"))
    capacity = max(4 * local_rows // owners, 2)
    slot_total = owners * capacity
    tile_rows = min(512, slot_total)
    block_count = slot_total // tile_rows
    unit = unit_rows(embeddings)
    cluster = assignment[:, 0]
    onehot = (cluster[:, None] == jnp.arange(owners, dtype=jnp.int32)[None, :]).astype(jnp.int32)
    slot_rank = jnp.sum((jnp.cumsum(onehot, axis=0) - onehot) * onehot, axis=1)
    slot_index = cluster * capacity + slot_rank
    outgoing = jnp.zeros((slot_total, feature_width), jnp.bfloat16).at[slot_index].set(unit)
    occupied = jnp.zeros((slot_total,), jnp.int32).at[slot_index].set(1)
    incoming, arrived = (
        lax.all_to_all(
            outgoing.reshape(owners, capacity, feature_width),
            ("blk", "clus"),
            split_axis=0,
            concat_axis=0,
            tiled=True,
        ),
        lax.all_to_all(
            occupied.reshape(owners, capacity),
            ("blk", "clus"),
            split_axis=0,
            concat_axis=0,
            tiled=True,
        ),
    )
    incoming = incoming.reshape(slot_total, feature_width)
    arrived = arrived.reshape(slot_total)
    valid_weight = arrived.astype(jnp.float32)
    live_count = jnp.sum(valid_weight)

    def block_density(queries):
        return tile_density(queries, incoming, valid_weight)

    density = lax.map(
        block_density, incoming.reshape(block_count, tile_rows, feature_width)
    ).reshape(slot_total)
    slot_score = jnp.log(density / live_count)
    returned = lax.all_to_all(
        slot_score.reshape(owners, capacity),
        ("blk", "clus"),
        split_axis=0,
        concat_axis=0,
        tiled=True,
    )
    return returned.reshape(slot_total)[slot_index]


def solution(mesh):
    placed = (P(("parts", "blk", "clus"), None), P(("parts", "blk", "clus"), None))
    sizes = (mesh.shape["parts"], mesh.shape["blk"], mesh.shape["clus"])
    body = pair_scores if sizes == (2, 8, 2) else routed_scores
    return jax.shard_map(
        body,
        mesh=mesh,
        in_specs=placed,
        out_specs=P(("parts", "blk", "clus")),
        check_vma=False,
    )
```

```python
import functools

import jax
import jax.numpy as jnp
from jax import lax
from jax.experimental import pallas as pl
from jax.experimental.pallas import tpu as pltpu
from jax.sharding import PartitionSpec as P

kernel_scale = 4.0
MESH = pl.DeviceIdType.MESH
CHUNKS = 8
ROUNDS = 11
RELAYED = 6
HALF = 256
LANES = 128
JOBS = (
    ((1, 0, 0, 0), (2, 0, 1, 0), (9, 0, 0, 1), (10, 0, 1, 1)),
    ((1, 1, 0, 0), (2, 1, 1, 0), (8, 0, 0, 0), (9, 1, 0, 1), (9, 1, 1, 1), (10, 0, 0, 1), (10, 0, 1, 0), (10, 0, 1, 1)),
    ((1, 2, 0, 0), (2, 2, 1, 0), (5, 1, 0, 0), (7, 3, 0, 0), (8, 0, 0, 0), (9, 1, 1, 0), (9, 2, 0, 1), (9, 2, 1, 1),
     (10, 1, 0, 1), (10, 1, 1, 1), (10, 3, 0, 1), (10, 0, 0, 1), (10, 3, 1, 0), (10, 3, 1, 1), (10, 0, 1, 0), (10, 0, 1, 1)),
    ((1, 3, 0, 0), (2, 3, 1, 0), (7, 1, 0, 0), (8, 1, 1, 0), (9, 3, 0, 1), (9, 3, 1, 1), (9, 1, 0, 1), (10, 1, 1, 1),
     (10, 0, 0, 0), (10, 0, 0, 1), (10, 0, 1, 0), (10, 0, 1, 1)),
)


def pick(table, index):
    value = jnp.int32(table[-1])
    for k in reversed(range(len(table) - 1)):
        value = jnp.where(index == k, table[k], value)
    return value


def pick_level(tables, level, index):
    return pick([pick(t, index) for t in tables], level)


def unit_rows(embeddings):
    widened = embeddings.astype(jnp.float32)
    normed = (
        widened
        * lax.rsqrt(jnp.mean(widened * widened, axis=1, keepdims=True) + 1e-06)
        * embeddings.shape[1] ** (-0.5)
    )
    return normed.astype(jnp.bfloat16)


def pair_kernel(
    emb_ref, id_ref, out_ref,
    line, plane, relay, ids, id_cols, row_acc, line_part, plane_part, gathered,
    line_send, line_recv, plane_send, plane_recv, id_send, id_recv, part_send, part_recv,
    relay_send, relay_recv, x_send,
):
    tok, width = emb_ref.shape
    rows = tok // CHUNKS
    part, blk, core = lax.axis_index("parts"), lax.axis_index("blk"), lax.axis_index("clus")
    z, y = blk // 2, blk % 2
    flip = 1 - 2 * part
    level = 3 * part + flip * z
    me = blk * 2 + core
    spot = y * 2 + core

    def at_level(other, oy=None, ocore=None):
        oz = 3 * part + flip * other
        return (part, oz * 2 + (y if oy is None else oy), core if ocore is None else ocore)

    def span(c):
        return pl.ds(pl.multiple_of(c * rows, rows), rows)

    def line_copy(source, c, target):
        return pltpu.make_async_remote_copy(
            src_ref=line.at[source, span(c)], dst_ref=line.at[source, span(c)],
            send_sem=line_send.at[source, c], recv_sem=line_recv.at[source, c],
            device_id=at_level(target), device_id_type=MESH)

    def plane_copy(kind, slot, c, target):
        return pltpu.make_async_remote_copy(
            src_ref=plane.at[slot, span(c)], dst_ref=plane.at[slot, span(c)],
            send_sem=plane_send.at[kind, c], recv_sem=plane_recv.at[slot, c],
            device_id=target, device_id_type=MESH)

    y_peer = at_level(level, oy=1 - y)
    c_peer = at_level(level, ocore=1 - core)
    y_spot = (1 - y) * 2 + core
    c_spot = y * 2 + 1 - core
    d_spot = (1 - y) * 2 + 1 - core

    barrier = pltpu.get_barrier_semaphore()

    def other(k):
        dev = (me + k) % 16
        return dev, (part, dev // 2, dev % 2)

    @pl.loop(1, 16)
    def _(k):
        pl.semaphore_signal(barrier, inc=1, device_id=other(k)[1], device_id_type=MESH)

    x_peer = (1 - part, blk, core)
    pl.semaphore_signal(barrier, inc=1, device_id=x_peer, device_id_type=MESH)
    ids[me] = id_ref[...]
    line_part[...] = jnp.zeros_like(line_part)
    row_acc[...] = jnp.zeros_like(row_acc)
    pl.semaphore_wait(barrier, 16)

    def id_copy(dev, at):
        return pltpu.make_async_remote_copy(
            src_ref=ids.at[me], dst_ref=ids.at[me],
            send_sem=id_send.at[dev], recv_sem=id_recv.at[me],
            device_id=at, device_id_type=MESH)

    def id_arrival(dev):
        return pltpu.make_async_remote_copy(
            src_ref=ids.at[dev], dst_ref=ids.at[dev],
            send_sem=id_send.at[dev], recv_sem=id_recv.at[dev],
            device_id=other(1)[1], device_id_type=MESH)

    @pl.loop(1, 16)
    def _(k):
        dev, at = other(k)
        id_copy(dev, at).start()

    def up_copy(i):
        first = (level == 0) | (i < 4)
        source = jnp.where(first, jnp.minimum(level, 1), 0)
        return line_copy(source, jnp.where(first, i, i - 4), level + 1)

    def up_round(r):
        i = r - level // 2

        @pl.when((level < 3) & (i >= 0) & (i < jnp.where(level == 0, 8, 10)))
        def _():
            @pl.when((level == 2) | ((level == 1) & (i >= 4)))
            def _():
                up_copy(i).wait_recv()

            @pl.when(i > 0)
            def _():
                up_copy(i - 1).wait_send()
            up_copy(i).start()

    def relay_copy(j):
        return pltpu.make_async_remote_copy(
            src_ref=relay.at[j], dst_ref=relay.at[j],
            send_sem=relay_send.at[j], recv_sem=relay_recv.at[j],
            device_id=at_level(level - 1), device_id_type=MESH)

    def down_round(r):
        @pl.when((level == 3) & (r < 10))
        def _():
            own = jnp.where(r < 2, r, r - 2)

            @pl.when((r == 2) | (r == 3))
            def _():
                @pl.when(r == 2)
                def _():
                    line_copy(3, 1, 2).wait_send()

                @pl.when(r == 3)
                def _():
                    relay_copy(4).wait_send()
                relay_copy(r + 2).wait_recv()
                relay_copy(r + 2).start()

            @pl.when((r < 2) | (r > 3))
            def _():
                @pl.when(r == 4)
                def _():
                    relay_copy(5).wait_send()

                @pl.when((r == 1) | (r > 4))
                def _():
                    line_copy(3, own - 1, 2).wait_send()
                line_copy(3, own, 2).start()

        i = r - (3 - level)

        @pl.when(((level == 1) | (level == 2)) & (i >= 0) & (i < RELAYED))
        def _():
            relay_copy(i).wait_recv()

            @pl.when(i > 0)
            def _():
                relay_copy(i - 1).wait_send()
            relay_copy(i).start()

    def out_copy(i):
        j = jnp.where(level == 0, 4 + i, i)
        return pltpu.make_async_remote_copy(
            src_ref=line.at[level, span(jnp.where(level == 0, 6 + i, 4 + i))], dst_ref=relay.at[j],
            send_sem=x_send.at[i], recv_sem=relay_recv.at[j],
            device_id=x_peer, device_id_type=MESH)

    def back_copy(i):
        j = jnp.where(level == 0, i - 2, i - 4)
        source = jnp.where(j < 4, 1, 0)
        at = span(jnp.where(j < 4, j + 4, j + 2))
        return pltpu.make_async_remote_copy(
            src_ref=relay.at[j], dst_ref=line.at[source, at],
            send_sem=x_send.at[i], recv_sem=line_recv.at[source, jnp.where(j < 4, j + 4, j + 2)],
            device_id=x_peer, device_id_type=MESH)

    def x_round(r):
        i = jnp.where((level == 0) & (r > 1), r - 1, r)
        outs = jnp.where(level == 0, 2, 4)
        total = jnp.where(level == 0, 8, 10)

        @pl.when((level < 2) & (i < total) & ((level == 1) | (r != 2)))
        def _():
            @pl.when(i > outs)
            def _():
                back_copy(i - 1).wait_send()

            @pl.when((i > 0) & (i <= outs))
            def _():
                out_copy(i - 1).wait_send()

            @pl.when(i < outs)
            def _():
                out_copy(i).start()

            @pl.when(i >= outs)
            def _():
                @pl.when(level == 0)
                def _():
                    relay_copy(i - 2).wait_recv()
                back_copy(i).start()

    def y_round(r):
        @pl.when(r < CHUNKS)
        def _():
            @pl.when(r > 0)
            def _():
                plane_copy(0, spot, r - 1, y_peer).wait_send()
            plane_copy(0, spot, r, y_peer).start()

    def y_pass(r):
        @pl.when((r > 0) & (r <= CHUNKS))
        def _():
            plane_copy(0, y_spot, r - 1, y_peer).wait_recv()
            plane_copy(2, y_spot, r - 1, c_peer).start()

    @pl.loop(0, CHUNKS)
    def _(c):
        unit = unit_rows(emb_ref[span(c), :])
        line[level, span(c)] = unit
        plane[spot, span(c)] = unit
        plane_copy(1, spot, c, c_peer).start()

    def comm(r):
        y_round(r)
        x_round(r)
        up_round(r)
        down_round(r)
        y_pass(r)

    comm(0)

    @pl.loop(1, 16)
    def _(k):
        id_arrival(other(k)[0]).wait_recv()

    @pl.loop(0, 4)
    def _(b):
        row = jnp.broadcast_to(ids[(blk - y) * 2 + b], (LANES, tok))
        id_cols[b] = row.T

    own_ids = id_ref[...]

    def count_cluster(d, total):
        col = jnp.broadcast_to(ids[d], (LANES, tok)).T
        parts = []
        for s in range(tok // LANES):
            same = col == own_ids[:, s * LANES:(s + 1) * LANES]
            parts.append(jnp.sum(jnp.where(same, 1.0, 0.0), axis=0, keepdims=True))
        return total + jnp.concatenate(parts, axis=1)

    count = lax.fori_loop(0, 16, count_cluster, jnp.zeros((1, tok), jnp.float32))

    steps = jnp.where(level == 0, 1, jnp.where(level == 1, 2, jnp.where(level == 2, 4, 3)))

    def source_of(t):
        at_two = jnp.where(t == 1, 1, jnp.where(t == 2, 3, 0))
        at_three = jnp.where(t == 1, 1, 0)
        later = jnp.where(level == 2, at_two, jnp.where(level == 3, at_three, 0))
        return jnp.where(t == 0, level, later)

    def part_copy(buffer, slot, sem, at):
        return pltpu.make_async_remote_copy(
            src_ref=buffer.at[slot], dst_ref=gathered.at[me],
            send_sem=part_send.at[sem], recv_sem=part_recv.at[me],
            device_id=at, device_id_type=MESH)

    starts = [[sum(1 for job in jobs if job[0] < r) for r in range(ROUNDS + 1)] for jobs in JOBS]

    def job(n):
        source = pick_level([[j[1] for j in jobs] for jobs in JOBS], level, n)
        h = pick_level([[j[2] for j in jobs] for jobs in JOBS], level, n)
        pair = pick_level([[j[3] for j in jobs] for jobs in JOBS], level, n)
        first = CHUNKS // 2 * h

        @pl.when((pair == 0) & (source != level))
        def _():
            everything = (level == 3) | (source == 3)
            low = jnp.where(everything, 0, jnp.where((source == 0) & (h == 1), 2, 0))
            high = jnp.where(everything | (h == 1), CHUNKS // 2, 0)

            @pl.loop(low, high)
            def _(c):
                line_copy(source, first + c, 0).wait_recv()

        src_dev = (3 * part + flip * source) * 4 + spot
        at = pl.ds(pl.multiple_of(h * HALF, HALF), HALF)
        id_row = ids[src_dev, :, at]

        def meet(k, total):
            b = (y + pair) % 2 * 2 + k
            gram = lax.dot_general(
                plane[b], line[source, at, :], (((1,), (1,)), ((), ())),
                preferred_element_type=jnp.float32)
            value = jnp.exp(kernel_scale * (gram - 1.0))
            col = id_cols[b]
            sums, rowsum = [], None
            for s in range(HALF // LANES):
                lanes = slice(s * LANES, (s + 1) * LANES)
                kept = jnp.where(col == id_row[:, lanes], value[:, lanes], 0.0)
                sums.append(jnp.sum(kept, axis=0, keepdims=True))
                rowsum = kept if rowsum is None else rowsum + kept

            @pl.when(source != level)
            def _():
                row_acc[b] = row_acc[b] + rowsum
            return total + jnp.concatenate(sums, axis=1)

        line_part[source, :, at] = line_part[source, :, at] + lax.fori_loop(
            0, 2, meet, jnp.zeros((1, HALF), jnp.float32))

    @pl.loop(1, ROUNDS)
    def _(r):
        comm(r)

        @pl.when(r == 1)
        def _():
            @pl.loop(0, CHUNKS)
            def _(c):
                plane_copy(1, c_spot, c, c_peer).wait_recv()

        @pl.when(r == 9)
        def _():
            @pl.loop(0, CHUNKS)
            def _(c):
                plane_copy(2, d_spot, c, c_peer).wait_recv()

        @pl.loop(pick_level(starts, level, r), pick_level(starts, level, r + 1))
        def _(n):
            job(n)

    @pl.loop(1, steps)
    def _(t):
        source = source_of(t)
        part_copy(line_part, source, source, at_level(source)).start()

    def plane_peer(k):
        peer = (spot + k) % 4
        return peer, at_level(level, oy=peer // 2, ocore=peer % 2)

    @pl.when(level > 0)
    def _():
        for b in range(4):
            plane_part[b] = jnp.sum(row_acc[b].T, axis=0, keepdims=True)
        for k in range(1, 4):
            peer, at = plane_peer(k)
            part_copy(plane_part, peer, 4 + peer, at).start()

    total = line_part[level]
    out_ref[...] = total

    def part_arrival(dev):
        return pltpu.make_async_remote_copy(
            src_ref=line_part.at[0], dst_ref=gathered.at[dev],
            send_sem=part_send.at[0], recv_sem=part_recv.at[dev],
            device_id=y_peer, device_id_type=MESH)

    def take(source_level):
        dev = (3 * part + flip * source_level) * 4 + spot
        part_arrival(dev).wait_recv()
        out_ref[...] = out_ref[...] + gathered[dev]

    @pl.when(level == 0)
    def _():
        take(1)

    @pl.when((level != 2))
    def _():
        take(2)

    @pl.when(level < 2)
    def _():
        take(3)

    @pl.when(level > 0)
    def _():
        out_ref[...] = out_ref[...] + plane_part[spot]
        for k in range(1, 4):
            dev = (blk - y) * 2 + plane_peer(k)[0]
            part_arrival(dev).wait_recv()
            out_ref[...] = out_ref[...] + gathered[dev]

    out_ref[...] = jnp.log(out_ref[...] / count)

    @pl.loop(1, 16)
    def _(k):
        dev, at = other(k)
        id_copy(dev, at).wait_send()

    @pl.loop(0, CHUNKS)
    def _(c):
        plane_copy(1, spot, c, c_peer).wait_send()
        plane_copy(2, y_spot, c, c_peer).wait_send()
    plane_copy(0, spot, CHUNKS - 1, y_peer).wait_send()

    @pl.when(level < 3)
    def _():
        up_copy(jnp.where(level == 0, 7, 9)).wait_send()

    @pl.when(level == 3)
    def _():
        line_copy(3, CHUNKS - 1, 2).wait_send()

    @pl.when((level == 1) | (level == 2))
    def _():
        relay_copy(RELAYED - 1).wait_send()

    @pl.when(level < 2)
    def _():
        back_copy(jnp.where(level == 0, 7, 9)).wait_send()

    @pl.loop(1, steps)
    def _(t):
        source = source_of(t)
        part_copy(line_part, source, source, at_level(source)).wait_send()

    @pl.when(level > 0)
    def _():
        for k in range(1, 4):
            peer, at = plane_peer(k)
            part_copy(plane_part, peer, 4 + peer, at).wait_send()


def pair_scores(embeddings, assignment):
    tok, width = embeddings.shape
    score = pl.pallas_call(
        pair_kernel,
        out_shape=jax.ShapeDtypeStruct((1, tok), jnp.float32),
        in_specs=[pl.BlockSpec(memory_space=pltpu.VMEM)] * 2,
        out_specs=pl.BlockSpec(memory_space=pltpu.VMEM),
        scratch_shapes=[
            pltpu.VMEM((4, tok, width), jnp.bfloat16),
            pltpu.VMEM((4, tok, width), jnp.bfloat16),
            pltpu.VMEM((RELAYED, tok // CHUNKS, width), jnp.bfloat16),
            pltpu.VMEM((16, 1, tok), jnp.int32),
            pltpu.VMEM((4, tok, LANES), jnp.int32),
            pltpu.VMEM((4, tok, LANES), jnp.float32),
            pltpu.VMEM((4, 1, tok), jnp.float32),
            pltpu.VMEM((4, 1, tok), jnp.float32),
            pltpu.VMEM((16, 1, tok), jnp.float32),
            pltpu.SemaphoreType.DMA((4, CHUNKS)),
            pltpu.SemaphoreType.DMA((4, CHUNKS)),
            pltpu.SemaphoreType.DMA((3, CHUNKS)),
            pltpu.SemaphoreType.DMA((4, CHUNKS)),
            pltpu.SemaphoreType.DMA((16,)),
            pltpu.SemaphoreType.DMA((16,)),
            pltpu.SemaphoreType.DMA((8,)),
            pltpu.SemaphoreType.DMA((16,)),
            pltpu.SemaphoreType.DMA((RELAYED,)),
            pltpu.SemaphoreType.DMA((RELAYED,)),
            pltpu.SemaphoreType.DMA((10,)),
        ],
        compiler_params=pltpu.CompilerParams(
            collective_id=0, has_side_effects=True, vmem_limit_bytes=40 << 20),
    )(embeddings, assignment.reshape(1, tok))
    return score.reshape(tok)


def tile_density(queries, keys, key_weight):
    gram = lax.dot_general(
        queries, keys, (((1,), (1,)), ((), ())), preferred_element_type=jnp.float32
    )
    return jnp.sum(jnp.exp(kernel_scale * (gram - 1.0)) * key_weight[None, :], axis=1)


def routed_scores(embeddings, assignment):
    local_rows = embeddings.shape[0]
    feature_width = embeddings.shape[1]
    owners = lax.axis_size(("blk", "clus"))
    capacity = max(4 * local_rows // owners, 2)
    slot_total = owners * capacity
    tile_rows = min(512, slot_total)
    block_count = slot_total // tile_rows
    unit = unit_rows(embeddings)
    cluster = assignment[:, 0]
    onehot = (cluster[:, None] == jnp.arange(owners, dtype=jnp.int32)[None, :]).astype(jnp.int32)
    slot_rank = jnp.sum((jnp.cumsum(onehot, axis=0) - onehot) * onehot, axis=1)
    slot_index = cluster * capacity + slot_rank
    outgoing = jnp.zeros((slot_total, feature_width), jnp.bfloat16).at[slot_index].set(unit)
    occupied = jnp.zeros((slot_total,), jnp.int32).at[slot_index].set(1)
    incoming, arrived = (
        lax.all_to_all(
            outgoing.reshape(owners, capacity, feature_width),
            ("blk", "clus"),
            split_axis=0,
            concat_axis=0,
            tiled=True,
        ),
        lax.all_to_all(
            occupied.reshape(owners, capacity),
            ("blk", "clus"),
            split_axis=0,
            concat_axis=0,
            tiled=True,
        ),
    )
    incoming = incoming.reshape(slot_total, feature_width)
    arrived = arrived.reshape(slot_total)
    valid_weight = arrived.astype(jnp.float32)
    live_count = jnp.sum(valid_weight)

    def block_density(queries):
        return tile_density(queries, incoming, valid_weight)

    density = lax.map(
        block_density, incoming.reshape(block_count, tile_rows, feature_width)
    ).reshape(slot_total)
    slot_score = jnp.log(density / live_count)
    returned = lax.all_to_all(
        slot_score.reshape(owners, capacity),
        ("blk", "clus"),
        split_axis=0,
        concat_axis=0,
        tiled=True,
    )
    return returned.reshape(slot_total)[slot_index]


def solution(mesh):
    placed = (P(("parts", "blk", "clus"), None), P(("parts", "blk", "clus"), None))
    sizes = (mesh.shape["parts"], mesh.shape["blk"], mesh.shape["clus"])
    body = pair_scores if sizes == (2, 8, 2) else routed_scores
    return jax.shard_map(
        body,
        mesh=mesh,
        in_specs=placed,
        out_specs=P(("parts", "blk", "clus")),
        check_vma=False,
    )
```

```python
import functools
import math

import jax
import jax.numpy as jnp
from jax import lax
from jax.experimental import pallas as pl
from jax.experimental.pallas import tpu as pltpu
from jax.sharding import PartitionSpec as P

kernel_scale = 4.0
MESH = pl.DeviceIdType.MESH
CHUNKS = 8
ROUNDS = 11
DEPTH = 2
RELAYED = 6
HALF = 256
LANES = 128
JOBS = (
    ((1, 0, 0, 0), (2, 0, 1, 0), (9, 0, 0, 1), (10, 0, 1, 1)),
    ((1, 1, 0, 0), (2, 1, 1, 0), (8, 0, 0, 0), (9, 1, 0, 1), (9, 1, 1, 1), (10, 0, 0, 1), (10, 0, 1, 0), (10, 0, 1, 1)),
    ((1, 2, 0, 0), (2, 2, 1, 0), (5, 1, 0, 0), (7, 3, 0, 0), (8, 0, 0, 0), (9, 1, 1, 0), (9, 2, 0, 1), (9, 2, 1, 1),
     (10, 1, 0, 1), (10, 1, 1, 1), (10, 3, 0, 1), (10, 0, 0, 1), (10, 3, 1, 0), (10, 3, 1, 1), (10, 0, 1, 0), (10, 0, 1, 1)),
    ((1, 3, 0, 0), (2, 3, 1, 0), (7, 1, 0, 0), (8, 1, 1, 0), (9, 3, 0, 1), (9, 3, 1, 1), (9, 1, 0, 1), (10, 1, 1, 1),
     (10, 0, 0, 0), (10, 0, 0, 1), (10, 0, 1, 0), (10, 0, 1, 1)),
)


def pick(table, index):
    value = jnp.int32(table[-1])
    for k in reversed(range(len(table) - 1)):
        value = jnp.where(index == k, table[k], value)
    return value


def pick_level(tables, level, index):
    return pick([pick(t, index) for t in tables], level)


def unit_rows(embeddings):
    widened = embeddings.astype(jnp.float32)
    normed = (
        widened
        * lax.rsqrt(jnp.mean(widened * widened, axis=1, keepdims=True) + 1e-06)
        * embeddings.shape[1] ** (-0.5)
    )
    return normed.astype(jnp.bfloat16)


def pair_kernel(
    emb_hbm, id_hbm, out_ref,
    emb_ref, id_ref, line, plane, relay, count_ref, ids, id_cols, row_acc, line_part, plane_part, gathered,
    line_send, line_recv, plane_send, plane_recv, id_send, id_recv, part_send, part_recv,
    relay_send, relay_recv, x_send, load_sem,
):
    tok, width = emb_ref.shape
    load_ids = pltpu.make_async_copy(id_hbm, id_ref, load_sem.at[0])
    load_rows = pltpu.make_async_copy(emb_hbm, emb_ref, load_sem.at[1])
    load_ids.start()
    load_rows.start()
    rows = tok // CHUNKS
    part, blk, core = lax.axis_index("parts"), lax.axis_index("blk"), lax.axis_index("clus")
    z, y = blk // 2, blk % 2
    flip = 1 - 2 * part
    level = 3 * part + flip * z
    me = blk * 2 + core
    spot = y * 2 + core

    def at_level(other, oy=None, ocore=None):
        oz = 3 * part + flip * other
        return (part, oz * 2 + (y if oy is None else oy), core if ocore is None else ocore)

    def span(c):
        return pl.ds(pl.multiple_of(c * rows, rows), rows)

    def plane_span(slot, c):
        return pl.ds(pl.multiple_of(slot * tok + c * rows, rows), rows)

    def line_copy(source, c, target):
        return pltpu.make_async_remote_copy(
            src_ref=line.at[source, span(c)], dst_ref=line.at[source, span(c)],
            send_sem=line_send.at[source, c], recv_sem=line_recv.at[source, c],
            device_id=at_level(target), device_id_type=MESH)

    def plane_copy(kind, slot, c, target):
        return pltpu.make_async_remote_copy(
            src_ref=plane.at[plane_span(slot, c)], dst_ref=plane.at[plane_span(slot, c)],
            send_sem=plane_send.at[kind, c], recv_sem=plane_recv.at[slot, c],
            device_id=target, device_id_type=MESH)

    y_peer = at_level(level, oy=1 - y)
    c_peer = at_level(level, ocore=1 - core)
    y_spot = (1 - y) * 2 + core
    c_spot = y * 2 + 1 - core
    d_spot = (1 - y) * 2 + 1 - core

    barrier = pltpu.get_barrier_semaphore()

    def other(k):
        dev = (me + k) % 16
        return dev, (part, dev // 2, dev % 2)

    @pl.loop(1, 16)
    def _(k):
        pl.semaphore_signal(barrier, inc=1, device_id=other(k)[1], device_id_type=MESH)

    x_peer = (1 - part, blk, core)
    pl.semaphore_signal(barrier, inc=1, device_id=x_peer, device_id_type=MESH)
    load_ids.wait()
    ids[me] = id_ref[...]
    line_part[...] = jnp.zeros_like(line_part)
    row_acc[...] = jnp.zeros_like(row_acc)
    load_rows.wait()

    @pl.loop(0, CHUNKS)
    def _(c):
        unit = unit_rows(emb_ref[span(c), :])
        line[level, span(c)] = unit
        plane[plane_span(spot, c)] = unit

    pl.semaphore_wait(barrier, 16)

    def id_copy(dev, at):
        return pltpu.make_async_remote_copy(
            src_ref=ids.at[me], dst_ref=ids.at[me],
            send_sem=id_send.at[dev], recv_sem=id_recv.at[me],
            device_id=at, device_id_type=MESH)

    def id_arrival(dev):
        return pltpu.make_async_remote_copy(
            src_ref=ids.at[dev], dst_ref=ids.at[dev],
            send_sem=id_send.at[dev], recv_sem=id_recv.at[dev],
            device_id=other(1)[1], device_id_type=MESH)

    @pl.loop(1, 16)
    def _(k):
        dev, at = other(k)
        id_copy(dev, at).start()

    def up_copy(i):
        first = (level == 0) | (i < 4)
        source = jnp.where(first, jnp.minimum(level, 1), 0)
        return line_copy(source, jnp.where(first, i, i - 4), level + 1)

    def up_round(r):
        i = r - level // 2

        @pl.when((level < 3) & (i >= 0) & (i < jnp.where(level == 0, 8, 10)))
        def _():
            @pl.when((level == 2) | ((level == 1) & (i >= 4)))
            def _():
                up_copy(i).wait_recv()

            @pl.when(i >= DEPTH)
            def _():
                up_copy(i - DEPTH).wait_send()
            up_copy(i).start()

    def relay_copy(j):
        return pltpu.make_async_remote_copy(
            src_ref=relay.at[j], dst_ref=relay.at[j],
            send_sem=relay_send.at[j], recv_sem=relay_recv.at[j],
            device_id=at_level(level - 1), device_id_type=MESH)

    def own_down(i):
        return line_copy(3, jnp.where(i < 2, i, i - 2), 2)

    def down_sent(i):
        passed = (i == 2) | (i == 3)

        @pl.when(passed)
        def _():
            relay_copy(i + 2).wait_send()

        @pl.when(jnp.logical_not(passed))
        def _():
            own_down(i).wait_send()

    def down_round(r):
        @pl.when((level == 3) & (r < 10))
        def _():
            passed = (r == 2) | (r == 3)

            @pl.when(passed)
            def _():
                relay_copy(r + 2).wait_recv()

            @pl.when(r >= DEPTH)
            def _():
                down_sent(r - DEPTH)

            @pl.when(passed)
            def _():
                relay_copy(r + 2).start()

            @pl.when(jnp.logical_not(passed))
            def _():
                own_down(r).start()

        i = r - (3 - level)

        @pl.when(((level == 1) | (level == 2)) & (i >= 0) & (i < RELAYED))
        def _():
            relay_copy(i).wait_recv()

            @pl.when(i >= DEPTH)
            def _():
                relay_copy(i - DEPTH).wait_send()
            relay_copy(i).start()

    def out_copy(i):
        j = jnp.where(level == 0, 4 + i, i)
        return pltpu.make_async_remote_copy(
            src_ref=line.at[level, span(jnp.where(level == 0, 6 + i, 4 + i))], dst_ref=relay.at[j],
            send_sem=x_send.at[i], recv_sem=relay_recv.at[j],
            device_id=x_peer, device_id_type=MESH)

    def back_copy(i):
        j = jnp.where(level == 0, i - 2, i - 4)
        source = jnp.where(j < 4, 1, 0)
        at = span(jnp.where(j < 4, j + 4, j + 2))
        return pltpu.make_async_remote_copy(
            src_ref=relay.at[j], dst_ref=line.at[source, at],
            send_sem=x_send.at[i], recv_sem=line_recv.at[source, jnp.where(j < 4, j + 4, j + 2)],
            device_id=x_peer, device_id_type=MESH)

    def x_sent(i):
        pltpu.make_async_remote_copy(
            src_ref=relay.at[0], dst_ref=relay.at[0],
            send_sem=x_send.at[i], recv_sem=relay_recv.at[0],
            device_id=x_peer, device_id_type=MESH).wait_send()

    def x_round(r):
        i = jnp.where((level == 0) & (r > 1), r - 1, r)
        outs = jnp.where(level == 0, 2, 4)
        total = jnp.where(level == 0, 8, 10)

        @pl.when((level < 2) & (i < total) & ((level == 1) | (r != 2)))
        def _():
            @pl.when(i >= DEPTH)
            def _():
                x_sent(i - DEPTH)

            @pl.when(i < outs)
            def _():
                out_copy(i).start()

            @pl.when(i >= outs)
            def _():
                @pl.when(level == 0)
                def _():
                    relay_copy(i - 2).wait_recv()
                back_copy(i).start()

    def y_round(r):
        @pl.when(r < CHUNKS)
        def _():
            @pl.when(r >= DEPTH)
            def _():
                plane_copy(0, spot, r - DEPTH, y_peer).wait_send()
            plane_copy(0, spot, r, y_peer).start()

    def y_pass(r):
        @pl.when((r > 0) & (r <= CHUNKS))
        def _():
            plane_copy(0, y_spot, r - 1, y_peer).wait_recv()
            plane_copy(2, y_spot, r - 1, c_peer).start()

    @pl.loop(0, CHUNKS)
    def _(c):
        plane_copy(1, spot, c, c_peer).start()

    def comm(r):
        y_round(r)
        x_round(r)
        up_round(r)
        down_round(r)
        y_pass(r)

    comm(0)

    @pl.loop(1, 16)
    def _(k):
        id_arrival(other(k)[0]).wait_recv()

    @pl.loop(0, 4)
    def _(b):
        row = jnp.broadcast_to(ids[(blk - y) * 2 + b], (LANES, tok))
        id_cols[pl.ds(pl.multiple_of(b * tok, tok), tok), :] = row.T

    own_ids = id_ref[...]

    def count_cluster(d, total):
        col = jnp.broadcast_to(ids[d], (LANES, tok)).T
        parts = []
        for s in range(tok // LANES):
            same = col == own_ids[:, s * LANES:(s + 1) * LANES]
            parts.append(jnp.sum(jnp.where(same, 1.0, 0.0), axis=0, keepdims=True))
        return total + jnp.concatenate(parts, axis=1)

    count_ref[...] = jnp.zeros_like(count_ref)

    steps = jnp.where(level == 0, 1, jnp.where(level == 1, 2, jnp.where(level == 2, 4, 3)))

    def source_of(t):
        at_two = jnp.where(t == 1, 1, jnp.where(t == 2, 3, 0))
        at_three = jnp.where(t == 1, 1, 0)
        later = jnp.where(level == 2, at_two, jnp.where(level == 3, at_three, 0))
        return jnp.where(t == 0, level, later)

    def part_copy(buffer, slot, sem, at):
        return pltpu.make_async_remote_copy(
            src_ref=buffer.at[slot], dst_ref=gathered.at[me],
            send_sem=part_send.at[sem], recv_sem=part_recv.at[me],
            device_id=at, device_id_type=MESH)

    starts = [[sum(1 for job in jobs if job[0] < r) for r in range(ROUNDS + 1)] for jobs in JOBS]

    def job(n):
        source = pick_level([[j[1] for j in jobs] for jobs in JOBS], level, n)
        h = pick_level([[j[2] for j in jobs] for jobs in JOBS], level, n)
        pair = pick_level([[j[3] for j in jobs] for jobs in JOBS], level, n)
        first = CHUNKS // 2 * h

        @pl.when((pair == 0) & (source != level))
        def _():
            everything = (level == 3) | (source == 3)
            low = jnp.where(everything, 0, jnp.where((source == 0) & (h == 1), 2, 0))
            high = jnp.where(everything | (h == 1), CHUNKS // 2, 0)

            @pl.loop(low, high)
            def _(c):
                line_copy(source, first + c, 0).wait_recv()

        src_dev = (3 * part + flip * source) * 4 + spot
        at = pl.ds(pl.multiple_of(h * HALF, HALF), HALF)
        id_row = ids[src_dev, :, at]

        two = pl.ds(pl.multiple_of((y + pair) % 2 * 2 * tok, 2 * tok), 2 * tok)
        gram = lax.dot_general(
            plane[two, :], line[source, at, :], (((1,), (1,)), ((), ())),
            preferred_element_type=jnp.float32)
        value = jnp.exp2((kernel_scale * math.log2(math.e)) * (gram - 1.0))
        col = id_cols[two, :]
        sums, rowsum = [], None
        for s in range(HALF // LANES):
            lanes = slice(s * LANES, (s + 1) * LANES)
            kept = jnp.where(col == id_row[:, lanes], value[:, lanes], 0.0)
            sums.append(jnp.sum(kept, axis=0, keepdims=True))
            rowsum = kept if rowsum is None else rowsum + kept

        @pl.when(source != level)
        def _():
            row_acc[two, :] = row_acc[two, :] + rowsum

        line_part[source, :, at] = line_part[source, :, at] + jnp.concatenate(sums, axis=1)

    @pl.loop(1, ROUNDS)
    def _(r):
        comm(r)

        @pl.when(r <= 8)
        def _():
            count_ref[...] = lax.fori_loop(2 * r - 2, 2 * r, count_cluster, count_ref[...])

        @pl.when(r == 1)
        def _():
            @pl.loop(0, CHUNKS)
            def _(c):
                plane_copy(1, c_spot, c, c_peer).wait_recv()

        @pl.when(r == 9)
        def _():
            @pl.loop(0, CHUNKS)
            def _(c):
                plane_copy(2, d_spot, c, c_peer).wait_recv()

        @pl.loop(pick_level(starts, level, r), pick_level(starts, level, r + 1))
        def _(n):
            job(n)

    @pl.loop(1, steps)
    def _(t):
        source = source_of(t)
        part_copy(line_part, source, source, at_level(source)).start()

    def plane_peer(k):
        peer = (spot + k) % 4
        return peer, at_level(level, oy=peer // 2, ocore=peer % 2)

    @pl.when(level > 0)
    def _():
        for b in range(4):
            plane_part[b] = jnp.sum(row_acc[b * tok:(b + 1) * tok, :].T, axis=0, keepdims=True)
        for k in range(1, 4):
            peer, at = plane_peer(k)
            part_copy(plane_part, peer, 4 + peer, at).start()

    total = line_part[level]
    out_ref[...] = total

    def part_arrival(dev):
        return pltpu.make_async_remote_copy(
            src_ref=line_part.at[0], dst_ref=gathered.at[dev],
            send_sem=part_send.at[0], recv_sem=part_recv.at[dev],
            device_id=y_peer, device_id_type=MESH)

    def take(source_level):
        dev = (3 * part + flip * source_level) * 4 + spot
        part_arrival(dev).wait_recv()
        out_ref[...] = out_ref[...] + gathered[dev]

    @pl.when(level == 0)
    def _():
        take(1)

    @pl.when((level != 2))
    def _():
        take(2)

    @pl.when(level < 2)
    def _():
        take(3)

    @pl.when(level > 0)
    def _():
        out_ref[...] = out_ref[...] + plane_part[spot]
        for k in range(1, 4):
            dev = (blk - y) * 2 + plane_peer(k)[0]
            part_arrival(dev).wait_recv()
            out_ref[...] = out_ref[...] + gathered[dev]

    out_ref[...] = jnp.log(out_ref[...] / count_ref[...])

    @pl.loop(1, 16)
    def _(k):
        dev, at = other(k)
        id_copy(dev, at).wait_send()

    @pl.loop(0, CHUNKS)
    def _(c):
        plane_copy(1, spot, c, c_peer).wait_send()
        plane_copy(2, y_spot, c, c_peer).wait_send()

    @pl.loop(0, DEPTH)
    def _(k):
        plane_copy(0, spot, CHUNKS - 1 - k, y_peer).wait_send()

        @pl.when(level < 3)
        def _():
            up_copy(jnp.where(level == 0, 7, 9) - k).wait_send()

        @pl.when(level == 3)
        def _():
            down_sent(9 - k)

        @pl.when((level == 1) | (level == 2))
        def _():
            relay_copy(RELAYED - 1 - k).wait_send()

        @pl.when(level < 2)
        def _():
            x_sent(jnp.where(level == 0, 7, 9) - k)

    @pl.loop(1, steps)
    def _(t):
        source = source_of(t)
        part_copy(line_part, source, source, at_level(source)).wait_send()

    @pl.when(level > 0)
    def _():
        for k in range(1, 4):
            peer, at = plane_peer(k)
            part_copy(plane_part, peer, 4 + peer, at).wait_send()


def pair_scores(embeddings, assignment):
    tok, width = embeddings.shape
    score = pl.pallas_call(
        pair_kernel,
        out_shape=jax.ShapeDtypeStruct((1, tok), jnp.float32),
        in_specs=[pl.BlockSpec(memory_space=pl.ANY)] * 2,
        out_specs=pl.BlockSpec(memory_space=pltpu.VMEM),
        scratch_shapes=[
            pltpu.VMEM((tok, width), jnp.bfloat16),
            pltpu.VMEM((1, tok), jnp.int32),
            pltpu.VMEM((4, tok, width), jnp.bfloat16),
            pltpu.VMEM((4 * tok, width), jnp.bfloat16),
            pltpu.VMEM((RELAYED, tok // CHUNKS, width), jnp.bfloat16),
            pltpu.VMEM((1, tok), jnp.float32),
            pltpu.VMEM((16, 1, tok), jnp.int32),
            pltpu.VMEM((4 * tok, LANES), jnp.int32),
            pltpu.VMEM((4 * tok, LANES), jnp.float32),
            pltpu.VMEM((4, 1, tok), jnp.float32),
            pltpu.VMEM((4, 1, tok), jnp.float32),
            pltpu.VMEM((16, 1, tok), jnp.float32),
            pltpu.SemaphoreType.DMA((4, CHUNKS)),
            pltpu.SemaphoreType.DMA((4, CHUNKS)),
            pltpu.SemaphoreType.DMA((3, CHUNKS)),
            pltpu.SemaphoreType.DMA((4, CHUNKS)),
            pltpu.SemaphoreType.DMA((16,)),
            pltpu.SemaphoreType.DMA((16,)),
            pltpu.SemaphoreType.DMA((8,)),
            pltpu.SemaphoreType.DMA((16,)),
            pltpu.SemaphoreType.DMA((RELAYED,)),
            pltpu.SemaphoreType.DMA((RELAYED,)),
            pltpu.SemaphoreType.DMA((10,)),
            pltpu.SemaphoreType.DMA((2,)),
        ],
        compiler_params=pltpu.CompilerParams(
            collective_id=0, has_side_effects=True, vmem_limit_bytes=60 << 20),
    )(embeddings, assignment.reshape(1, tok))
    return score.reshape(tok)


def tile_density(queries, keys, key_weight):
    gram = lax.dot_general(
        queries, keys, (((1,), (1,)), ((), ())), preferred_element_type=jnp.float32
    )
    return jnp.sum(jnp.exp(kernel_scale * (gram - 1.0)) * key_weight[None, :], axis=1)


def routed_scores(embeddings, assignment):
    local_rows = embeddings.shape[0]
    feature_width = embeddings.shape[1]
    owners = lax.axis_size(("blk", "clus"))
    capacity = max(4 * local_rows // owners, 2)
    slot_total = owners * capacity
    tile_rows = min(512, slot_total)
    block_count = slot_total // tile_rows
    unit = unit_rows(embeddings)
    cluster = assignment[:, 0]
    onehot = (cluster[:, None] == jnp.arange(owners, dtype=jnp.int32)[None, :]).astype(jnp.int32)
    slot_rank = jnp.sum((jnp.cumsum(onehot, axis=0) - onehot) * onehot, axis=1)
    slot_index = cluster * capacity + slot_rank
    outgoing = jnp.zeros((slot_total, feature_width), jnp.bfloat16).at[slot_index].set(unit)
    occupied = jnp.zeros((slot_total,), jnp.int32).at[slot_index].set(1)
    incoming, arrived = (
        lax.all_to_all(
            outgoing.reshape(owners, capacity, feature_width),
            ("blk", "clus"),
            split_axis=0,
            concat_axis=0,
            tiled=True,
        ),
        lax.all_to_all(
            occupied.reshape(owners, capacity),
            ("blk", "clus"),
            split_axis=0,
            concat_axis=0,
            tiled=True,
        ),
    )
    incoming = incoming.reshape(slot_total, feature_width)
    arrived = arrived.reshape(slot_total)
    valid_weight = arrived.astype(jnp.float32)
    live_count = jnp.sum(valid_weight)

    def block_density(queries):
        return tile_density(queries, incoming, valid_weight)

    density = lax.map(
        block_density, incoming.reshape(block_count, tile_rows, feature_width)
    ).reshape(slot_total)
    slot_score = jnp.log(density / live_count)
    returned = lax.all_to_all(
        slot_score.reshape(owners, capacity),
        ("blk", "clus"),
        split_axis=0,
        concat_axis=0,
        tiled=True,
    )
    return returned.reshape(slot_total)[slot_index]


def solution(mesh):
    placed = (P(("parts", "blk", "clus"), None), P(("parts", "blk", "clus"), None))
    sizes = (mesh.shape["parts"], mesh.shape["blk"], mesh.shape["clus"])
    body = pair_scores if sizes == (2, 8, 2) else routed_scores
    return jax.shard_map(
        body,
        mesh=mesh,
        in_specs=placed,
        out_specs=P(("parts", "blk", "clus")),
        check_vma=False,
    )
```
